512 devices in a mesh: span: 64 (over y, z), ctx: 8 (over x, core).
Axes of the slice: x: 4, y: 4, z: 16, core: 2. Of those that a mesh axis runs over, the one named last changes fastest.
Arguments:
- queries: bfloat16 [64, 8192], P('span')
- ctx_keys: bfloat16 [64, 2048, 1024], P('span', 'ctx'), may hold values from -6 to 6
- ctx_values: bfloat16 [64, 2048, 1024], P('span', 'ctx'), may hold values from -6 to 6
- lengths: int32 [64], P('span'), may hold values from 1 to 2048
- new_key: bfloat16 [64, 1024], P('span', 'ctx')
- new_value: bfloat16 [64, 1024], P('span', 'ctx'), may hold values from -6 to 6
- span_keys: bfloat16 [256, 512, 1024], P('span', None, 'ctx'), may hold values from -6 to 6
- span_values: bfloat16 [256, 512, 1024], P('span', None, 'ctx'), may hold values from -6 to 6
- span_lists: int32 [64, 16], P('span'), may hold values from 0 to 255, as said below
- span_slots: int32 [256], replicated, may hold values from 0 to 255, as said below
Outputs:
- attended: bfloat16 [64, 8192], P('span', 'ctx')
The draws below stay inside these ranges and needn't reach their ends.
Inputs may be any that keep to these rules, and one draw needn't show every extreme that they name: `span_lists`: A slot s lies on index s // 4 of span, its holder. A request's 16 ids lie on 16 different holders; among the requests of one index of span, each holder is named at most once, and some holder exactly once. `span_slots`: each slot is named by exactly one id.
All inputs are finite; a program needn't handle non-finite values.
Results may differ from the reference program's by a relative error of at most 0.0095.
Values may be sent and summed in bfloat16 or wider, within the bound.
No kernel may reach another device: no remote copies, remote signals or barrier semaphores. Data moves between devices by JAX's collectives and lax.ppermute only.
A program may use at most 64 MiB of HBM per device.

```python
import jax
import jax.numpy as jnp
from jax import lax

HQ = 64
KVH = 8
DH = 128
SPAN_LEN = 512
TOP = 16
CH_DEV = 4
REQ_DEV = 1
SPANS = 256
REQUESTS = 64
CTXLEN = 2048
N_SPAN = 64


def shared_base(key):
    return jnp.clip(jax.random.normal(key, (REQUESTS, KVH * DH), jnp.float32), -4.0, 4.0)


def slot_table(key):
    return jax.random.permutation(jax.random.fold_in(key, 11), SPANS).astype(jnp.int32)


def draw_span_slots(key, part):
    table = slot_table(key)
    return table


def draw_span_lists(key, part):
    table = slot_table(key)
    key = jax.random.fold_in(key, 9)
    ident_of_slot = jnp.argsort(table).astype(jnp.int32)
    block_keys = jax.random.split(key, N_SPAN)
    holder_order = jax.vmap(lambda k: jax.random.permutation(k, N_SPAN).astype(jnp.int32))(block_keys)
    picks = jnp.arange(REQ_DEV * TOP, dtype=jnp.int32) % N_SPAN
    holders = holder_order[:, picks].reshape(REQUESTS, TOP)
    column = jax.random.randint(jax.random.fold_in(key, 2), (REQUESTS, TOP), 0, CH_DEV).astype(jnp.int32)
    slots = holders * CH_DEV + column
    return ident_of_slot[slots]


def draw_new_key(key, part):
    base = shared_base(key)
    return base.astype(jnp.bfloat16)


def draw_queries(key, part):
    key = jax.random.fold_in(key, 7)
    noise = jnp.clip(jax.random.normal(key, (REQUESTS, HQ * DH), jnp.float32), -4.0, 4.0)
    return noise.astype(jnp.bfloat16)


def place_ends(result, stream_key, low, high):
    longest = result.shape.index(max(result.shape))
    spots = []
    for shift in (0, 1):
        where = [jax.random.randint(jax.random.fold_in(stream_key, axis), (), 0, length) for axis, length in enumerate(result.shape)]
        where[longest] = (where[longest] + shift) % result.shape[longest]
        spots.append(tuple(where))
    return result.at[spots[0]].set(low).at[spots[1]].set(high)


def level_of(own_key, extent, cuts, low, high):
    loudness, own = 1.0, jax.random.fold_in(own_key, 6)
    for axis_at, blocks in cuts:
        heights = jnp.exp(jax.random.uniform(jax.random.fold_in(own, axis_at), (blocks,), jnp.float32, low / len(cuts), high / len(cuts)))
        loudness = loudness * jnp.repeat(heights, extent[axis_at] // blocks).reshape([-1 if axis == axis_at else 1 for axis in range(len(extent))])
    return loudness


def scatter_about(own_key, dims, spread, reach, pieces=(), held_as=jnp.bfloat16):
    entries = spread * jax.random.normal(own_key, dims, jnp.float32)
    if pieces:
        entries = entries * level_of(own_key, dims, pieces, -0.22, 0.18)
    return jnp.clip(entries, -reach, reach).astype(held_as)


def setup_inputs(seed: int = 0) -> dict:
    arg_keys = jax.random.split(jax.random.key(seed), 11)
    return {
        "queries": draw_queries(jax.random.fold_in(arg_keys[10], 71), 0),
        "ctx_keys": scatter_about(arg_keys[1], (REQUESTS, CTXLEN, KVH * DH), 1.0, 6.0, ((0, 64), (1, 8))),
        "ctx_values": scatter_about(arg_keys[2], (REQUESTS, CTXLEN, KVH * DH), 1.0, 6.0, ((0, 64), (1, 8))),
        "lengths": place_ends(jax.random.randint(arg_keys[3], (REQUESTS,), 1, CTXLEN + 1), jax.random.fold_in(arg_keys[3], 1), 1, CTXLEN).astype(jnp.int32),
        "new_key": draw_new_key(jax.random.fold_in(arg_keys[10], 71), 0),
        "new_value": scatter_about(arg_keys[5], (REQUESTS, KVH * DH), 1.0, 6.0, ((0, 64), (1, 8))),
        "span_keys": scatter_about(arg_keys[6], (SPANS, SPAN_LEN, KVH * DH), 1.0, 6.0, ((0, 64), (2, 8))),
        "span_values": scatter_about(arg_keys[7], (SPANS, SPAN_LEN, KVH * DH), 1.0, 6.0, ((0, 64), (2, 8))),
        "span_lists": draw_span_lists(jax.random.fold_in(arg_keys[10], 71), 0),
        "span_slots": draw_span_slots(jax.random.fold_in(arg_keys[10], 71), 0),
    }


def reference(queries, ctx_keys, ctx_values, lengths, new_key, new_value, span_keys, span_values, span_lists, span_slots):
    per_group = HQ // KVH
    scaling = 1.0 / (DH ** 0.5)

    def one_request(items):
        query, keys_priv, vals_priv, length, key_new, val_new, idents = items
        slots = span_slots[idents]
        keys_span = span_keys[slots].reshape(TOP * SPAN_LEN, KVH * DH)
        vals_span = span_values[slots].reshape(TOP * SPAN_LEN, KVH * DH)
        keys_all = jnp.concatenate([keys_priv, keys_span, key_new[None, :]], 0).astype(jnp.float32).reshape(-1, KVH, DH)
        vals_all = jnp.concatenate([vals_priv, vals_span, val_new[None, :]], 0).astype(jnp.float32).reshape(-1, KVH, DH)
        positions = jnp.arange(CTXLEN, dtype=jnp.int32)
        valid = jnp.concatenate([positions < length, jnp.ones((TOP * SPAN_LEN + 1,), bool)], 0)
        query_f = query.astype(jnp.float32).reshape(KVH, per_group, DH)
        scores = jnp.einsum('gqd,tgd->gqt', query_f, keys_all) * scaling
        scores = jnp.where(valid, scores, -1e30)
        peak = jnp.max(scores, -1, keepdims=True)
        weights = jnp.where(valid, jnp.exp(scores - peak), 0.0)
        total = jnp.sum(weights, -1)
        numer = jnp.einsum('gqt,tgd->gqd', weights, vals_all)
        return (numer / total[..., None]).reshape(HQ * DH).astype(jnp.bfloat16)

    return lax.map(one_request, (queries, ctx_keys, ctx_values, lengths, new_key, new_value, span_lists))
```

```python
import functools

import jax
import jax.numpy as jnp
from jax import lax
from jax.experimental import pallas as pl
from jax.experimental.pallas import tpu as pltpu
from jax.sharding import PartitionSpec as P

HQ = 64
KVH = 8
DH = 128
CORES = 2
LOW = -1e30
SCALE = 1.0 / DH**0.5
F32 = jnp.float32
BF16 = jnp.bfloat16


def swapped(value, mask):
    n = lax.axis_size("ctx")
    return lax.ppermute(value, "ctx", [(i, i ^ mask) for i in range(n)])


def exchanged(value):
    n = lax.axis_size("span")
    first = n * 7 // 16
    order = [(first + k) % n for k in range(n)]
    return lax.all_to_all(value, "span", 0, 0, axis_index_groups=[order], tiled=True)


def split(lse):
    high = lse.astype(BF16).astype(F32)
    rest = lse - high
    middle = rest.astype(BF16).astype(F32)
    return high, middle, rest - middle


def lanes(shape):
    return lax.broadcasted_iota(jnp.int32, shape, len(shape) - 1)


def spread(lse):
    lane = lanes(lse.shape[:-1] + (DH,))
    result = jnp.zeros(lane.shape, F32)
    for k, part in enumerate(split(lse)):
        result = jnp.where(lane == k, part, result)
    return result


def diagonals(shape):
    head = lax.broadcasted_iota(jnp.int32, shape, 1)
    return [lanes(shape) == head + 8 * k for k in range(3)]


def block_of(attended, lse):
    count = attended.shape[0]
    row = jnp.zeros(attended.shape, F32)
    for where, part in zip(diagonals(attended.shape), split(lse)):
        row = jnp.where(where, part, row)
    row = jnp.sum(row, 1, keepdims=True)
    row = jnp.broadcast_to(row, (count, 2, DH)).reshape(count, 1, 2, DH)
    return jnp.concatenate([attended.reshape(count, 4, 2, DH), row], 1).astype(BF16)


def fetch(pairs, sems):
    copies = [pltpu.make_async_copy(*pair, sems.at[k]) for k, pair in enumerate(pairs)]
    for copy in copies:
        copy.start()
    return copies


def pack_kernel(queries_ref, lists_ref, out_ref, held_ref, query_ref, ids_ref, sems):
    mine = lax.axis_index("ctx")
    width = KVH * DH
    part = queries_ref.at[:, pl.ds(pl.multiple_of(mine * width, width), width)]
    for copy in fetch(((part, query_ref), (lists_ref, ids_ref)), sems):
        copy.wait()
    query = query_ref[...].astype(F32)
    rows = [query[:, h * DH : (h + 1) * DH] for h in range(KVH)]
    ids = ids_ref[...].astype(F32)
    ids = jnp.concatenate([ids, jnp.full((1, DH - ids.shape[1]), -1.0, F32)], 1)
    block = jnp.concatenate(rows + [ids, ids], 0).reshape(5, 2, DH).astype(BF16)
    count = held_ref.shape[0]
    for copy in range(count):
        held_ref[copy] = block
    places = range(0, out_ref.shape[0], count)
    pairs = [(held_ref, out_ref.at[pl.ds(place, count)]) for place in places]
    for copy in fetch(pairs, sems):
        copy.wait()


def private_kernel(*refs):
    count = len(refs) // 2 - 2
    here_ref, there_ref, idents_ref = refs[count : count + 3]
    held, sems = refs[count + 3 : -1], refs[-1]
    copies = fetch(tuple(zip(refs[:count], held)), sems)
    lengths_ref, slots_ref, queries_ref, key_ref, value_ref, keys_ref, values_ref = held
    for copy in copies[:-1]:
        copy.wait()
    positions = keys_ref.shape[1]
    mine = lax.axis_index("ctx")
    first = mine * positions
    core = lax.rem(mine, CORES)
    chip = (mine - core) // CORES
    groups = [
        jnp.bitwise_xor(chip, step) * CORES + which
        for which in (core, 1 - core)
        for step in (0, 3, 1, 2)
    ]
    heads = [pl.ds(pl.multiple_of(g * DH, DH), DH) for g in groups]
    scores = []
    for k in range(KVH):
        width = 8 * DH
        mine_q = queries_ref[:, pl.ds(pl.multiple_of(groups[k] * width, width), width)]
        mine_q = mine_q.astype(F32)
        query = jnp.concatenate([mine_q[:, h * DH : (h + 1) * DH] for h in range(8)], 0)
        if k == 0:
            own = jnp.sum(query * key_ref[...].astype(F32), -1, keepdims=True) * SCALE
        scores.append(
            lax.dot_general(
                query.astype(BF16),
                keys_ref[0, :, heads[k]],
                (((1,), (1,)), ((), ())),
                preferred_element_type=F32,
            )
        )
    score = jnp.concatenate(scores, 0) * SCALE
    place = first + lax.broadcasted_iota(jnp.int32, score.shape, 1)
    valid = place < lengths_ref[0]
    score = jnp.where(valid, score, LOW)
    own = jnp.concatenate([own, jnp.full((HQ - 8, 1), LOW, F32)], 0)
    peak = jnp.maximum(jnp.max(score, -1, keepdims=True), own)
    weight = jnp.where(valid, jnp.exp(score - peak), 0.0)
    own = jnp.exp(own[:8] - peak[:8])
    total = jnp.sum(weight, -1, keepdims=True)
    total = jnp.concatenate([total[:8] + own, total[8:]], 0)
    some = total > 0.0
    safe = jnp.where(some, total, 1.0)
    stats = spread(jnp.where(some, peak + jnp.log(safe), LOW))
    weight = weight.astype(BF16)
    copies[-1].wait()
    for k in range(KVH):
        rows = slice(k * 8, k * 8 + 8)
        numer = jnp.dot(weight[rows], values_ref[0, :, heads[k]], preferred_element_type=F32)
        if k == 0:
            numer = numer + own * value_ref[...].astype(F32)
        message = jnp.concatenate([numer / safe[rows], stats[rows]], 0).astype(BF16)
        out_ref = here_ref if k < KVH // CORES else there_ref
        out_ref[k % (KVH // CORES)] = message
    table = slots_ref[...]
    number = (
        lax.broadcasted_iota(jnp.int32, table.shape, 0) * table.shape[1]
        + lax.broadcasted_iota(jnp.int32, table.shape, 1)
    )
    me = lax.axis_index("span")
    idents = []
    for column in range(idents_ref.shape[0]):
        found = jnp.where(table == me * idents_ref.shape[0] + column, number, 0)
        found = jnp.sum(jnp.sum(found, 0, keepdims=True), 1, keepdims=True)
        idents.append(jnp.broadcast_to(found, (1, DH)))
    idents_ref[...] = jnp.concatenate(idents, 0).astype(F32)


def span_kernel(gathered_ref, idents_ref, keys_ref, values_ref, out_ref):
    columns = keys_ref.shape[0]
    requests = gathered_ref.shape[0]
    count = min(32, requests)
    rows = count * 8
    keys = jnp.concatenate([keys_ref[column] for column in range(columns)], 1)
    values = jnp.concatenate([values_ref[column] for column in range(columns)], 1)
    for start in range(0, requests, count):
        message = gathered_ref[start : start + count].astype(F32)
        query = message[:, :4].reshape(rows, DH)
        ids = message[:, 4, :1, :]
        code = jnp.zeros_like(ids)
        for column in range(columns):
            ident = idents_ref[column : column + 1, :][None]
            code = jnp.where(ids == ident, column + 1.0, code)
        code = jnp.max(code, -1, keepdims=True)
        code = jnp.broadcast_to(code, (count, 8, DH)).reshape(rows, DH)
        listed = [code == column + 1.0 for column in range(columns)]
        query = jnp.concatenate([jnp.where(here, query, 0.0) for here in listed], 1)
        score = SCALE * lax.dot_general(
            query.astype(BF16), keys, (((1,), (1,)), ((), ())), preferred_element_type=F32
        )
        peak = jnp.max(score, -1, keepdims=True)
        weight = jnp.exp(score - peak)
        total = jnp.sum(weight, -1, keepdims=True)
        lse = jnp.where(code[:, :1] > 0.0, peak + jnp.log(total), LOW)
        numers = jnp.dot(weight.astype(BF16), values, preferred_element_type=F32)
        numer = jnp.zeros((rows, DH), F32)
        for column in range(columns):
            numer = jnp.where(listed[column], numers[:, column * DH : (column + 1) * DH], numer)
        attended = (numer / total).reshape(count, 8, DH)
        out_ref[start : start + count] = block_of(attended, lse.reshape(count, 8, 1))


def fold_kernel(first_ref, second_ref, *out_refs):
    parts = [first_ref[...].astype(F32), second_ref[...].astype(F32)]
    lses = [jnp.sum(part[:, 8:, :], -1, keepdims=True) for part in parts]
    peak = jnp.maximum(*lses)
    weights = [jnp.exp(lse - peak) for lse in lses]
    total = sum(weights)
    attended = sum(w * part[:, :8, :] for w, part in zip(weights, parts)) / total
    stats = spread(jnp.where(peak > LOW / 2, peak + jnp.log(total), LOW))
    result = jnp.concatenate([attended, stats], 1).astype(BF16)
    size = result.shape[0] // len(out_refs)
    for k, out_ref in enumerate(out_refs):
        out_ref[...] = result[k * size : (k + 1) * size]


def merge_kernel(spans_ref, here_ref, there_ref, out_ref):
    spans = spans_ref[...].astype(F32)
    attended = spans[:, :4].reshape(-1, 8, DH)
    row = jnp.broadcast_to(spans[:, 4, :1, :], attended.shape)
    kept = functools.reduce(jnp.logical_or, diagonals(attended.shape))
    lse = jnp.sum(jnp.where(kept, row, 0.0), -1, keepdims=True)
    tiles = [here_ref[0].astype(F32), there_ref[0].astype(F32)]
    lses = [jnp.sum(tile[8:], -1, keepdims=True) for tile in tiles]
    peak = functools.reduce(jnp.maximum, lses, jnp.max(lse, 0))
    weight = jnp.exp(lse - peak[None])
    weights = [jnp.exp(other - peak) for other in lses]
    total = sum(weights, jnp.sum(weight, 0))
    numer = sum(
        (w * tile[:8] for w, tile in zip(weights, tiles)), jnp.sum(weight * attended, 0)
    )
    result = numer / total
    out_ref[...] = jnp.concatenate([result[h : h + 1] for h in range(8)], 1).astype(BF16)


def vmem(count):
    return [pl.BlockSpec(memory_space=pltpu.VMEM)] * count


def hbm(count):
    return [pl.BlockSpec(memory_space=pltpu.HBM)] * count


def shards(
    queries,
    ctx_keys,
    ctx_values,
    lengths,
    new_key,
    new_value,
    span_keys,
    span_values,
    span_lists,
    span_slots,
):
    requests = lax.axis_size("span")
    chips = lax.axis_size("ctx") // CORES
    ch_dev = span_keys.shape[0]
    params = pltpu.CompilerParams(vmem_limit_bytes=16 * 1024 * 1024)
    alone = pltpu.CompilerParams(vmem_limit_bytes=56 * 1024 * 1024)
    blocks = jax.ShapeDtypeStruct((requests, 5, 2, DH), BF16)

    def tiles(count):
        return jax.ShapeDtypeStruct((count, 16, DH), BF16)

    def fold(here, there):
        return pl.pallas_call(
            fold_kernel,
            out_shape=[tiles(here.shape[0] // 2)] * 2,
            in_specs=vmem(2),
            out_specs=vmem(2),
            compiler_params=params,
            name="fold",
        )(here, there)

    packed = pl.pallas_call(
        pack_kernel,
        out_shape=blocks,
        in_specs=hbm(2),
        out_specs=hbm(1)[0],
        scratch_shapes=[
            pltpu.VMEM((requests // 4,) + blocks.shape[1:], BF16),
            pltpu.VMEM((1, KVH * DH), BF16),
            pltpu.VMEM(span_lists.shape, jnp.int32),
            pltpu.SemaphoreType.DMA((4,)),
        ],
        compiler_params=alone,
        name="pack",
    )(queries, span_lists)
    gathered = exchanged(packed)
    queries, packed = lax.optimization_barrier((queries, packed))
    table = span_slots.reshape(-1, min(DH, span_slots.shape[0]))
    fetched = (table, queries, new_key, new_value, ctx_keys, ctx_values)
    here, there, idents = pl.pallas_call(
        private_kernel,
        out_shape=[tiles(chips)] * CORES + [jax.ShapeDtypeStruct((ch_dev, DH), F32)],
        in_specs=hbm(1 + len(fetched)),
        out_specs=vmem(CORES + 1),
        scratch_shapes=[pltpu.SMEM(lengths.shape, jnp.int32)]
        + [pltpu.VMEM(array.shape, array.dtype) for array in fetched]
        + [pltpu.SemaphoreType.DMA((1 + len(fetched),))],
        compiler_params=alone,
        cost_estimate=pl.CostEstimate(
            flops=4 * HQ * ctx_keys.shape[1] * DH, bytes_accessed=1 << 20, transcendentals=1 << 14
        ),
        name="private",
    )(lengths, *fetched)
    there, gathered = lax.optimization_barrier((swapped(there, 1), gathered))
    partial = pl.pallas_call(
        span_kernel,
        out_shape=blocks,
        in_specs=vmem(4),
        out_specs=vmem(1)[0],
        compiler_params=params,
        cost_estimate=pl.CostEstimate(
            flops=4 * requests * 8 * DH * ch_dev * span_keys.shape[1],
            bytes_accessed=3 << 19,
            transcendentals=1 << 18,
        ),
        name="spans",
    )(gathered, idents, span_keys, span_values)
    partial = exchanged(partial)
    for mask in (1, 3):
        here, there = fold(here, there)
        there = swapped(there, mask * CORES)
    return pl.pallas_call(
        merge_kernel,
        out_shape=jax.ShapeDtypeStruct((1, KVH * DH), BF16),
        in_specs=vmem(3),
        out_specs=vmem(1)[0],
        compiler_params=params,
        name="merge",
    )(partial, here, there)


def solution(mesh):
    in_specs = (
        P("span", None),
        P("span", "ctx", None),
        P("span", "ctx", None),
        P("span"),
        P("span", "ctx"),
        P("span", "ctx"),
        P("span", None, "ctx"),
        P("span", None, "ctx"),
        P("span", None),
        P(),
    )
    out_specs = P("span", "ctx")
    return jax.shard_map(shards, mesh=mesh, in_specs=in_specs, out_specs=out_specs, check_vma=False)
```

```python
import functools

import jax
import jax.numpy as jnp
from jax import lax
from jax.experimental import pallas as pl
from jax.experimental.pallas import tpu as pltpu
from jax.sharding import PartitionSpec as P

HQ = 64
KVH = 8
DH = 128
CORES = 2
LOW = -1e30
SCALE = 1.0 / DH**0.5
LOG2E = 1.4426950408889634
F32 = jnp.float32
BF16 = jnp.bfloat16


def swapped(value, mask):
    n = lax.axis_size("ctx")
    return lax.ppermute(value, "ctx", [(i, i ^ mask) for i in range(n)])


def exchanged(value):
    n = lax.axis_size("span")
    first = n * 7 // 16
    order = [(first + k) % n for k in range(n)]
    return lax.all_to_all(value, "span", 0, 0, axis_index_groups=[order], tiled=True)


def split(lse):
    high = lse.astype(BF16).astype(F32)
    rest = lse - high
    middle = rest.astype(BF16).astype(F32)
    return high, middle, rest - middle


def lanes(shape):
    return lax.broadcasted_iota(jnp.int32, shape, len(shape) - 1)


def spread(lse):
    lane = lanes(lse.shape[:-1] + (DH,))
    result = jnp.zeros(lane.shape, F32)
    for k, part in enumerate(split(lse)):
        result = jnp.where(lane == k, part, result)
    return result


def diagonals(shape):
    head = lax.broadcasted_iota(jnp.int32, shape, 1)
    return [lanes(shape) == head + 8 * k for k in range(3)]


def block_of(attended, lse):
    count = attended.shape[0]
    row = jnp.zeros(attended.shape, F32)
    for where, part in zip(diagonals(attended.shape), split(lse)):
        row = jnp.where(where, part, row)
    row = jnp.sum(row, 1, keepdims=True)
    row = jnp.broadcast_to(row, (count, 2, DH)).reshape(count, 1, 2, DH)
    return jnp.concatenate([attended.reshape(count, 4, 2, DH), row], 1).astype(BF16)


def fetch(pairs, sems):
    copies = [pltpu.make_async_copy(*pair, sems.at[k]) for k, pair in enumerate(pairs)]
    for copy in copies:
        copy.start()
    return copies


def pack_kernel(queries_ref, lists_ref, out_ref, held_ref, query_ref, ids_ref, sems):
    mine = lax.axis_index("ctx")
    width = KVH * DH
    part = queries_ref.at[:, pl.ds(pl.multiple_of(mine * width, width), width)]
    for copy in fetch(((part, query_ref), (lists_ref, ids_ref)), sems):
        copy.wait()
    query = query_ref[...].astype(F32)
    rows = [query[:, h * DH : (h + 1) * DH] for h in range(KVH)]
    ids = ids_ref[...].astype(F32)
    ids = jnp.concatenate([ids, jnp.full((1, DH - ids.shape[1]), -1.0, F32)], 1)
    block = jnp.concatenate(rows + [ids, ids], 0).reshape(5, 2, DH).astype(BF16)
    count = held_ref.shape[0]
    for copy in range(count):
        held_ref[copy] = block
    places = range(0, out_ref.shape[0], count)
    pairs = [(held_ref, out_ref.at[pl.ds(place, count)]) for place in places]
    for copy in fetch(pairs, sems):
        copy.wait()


def private_kernel(*refs):
    count = len(refs) // 2 - 2
    here_ref, there_ref, idents_ref = refs[count : count + 3]
    held, sems = refs[count + 3 : -1], refs[-1]
    copies = fetch(tuple(zip(refs[:count], held)), sems)
    lengths_ref, slots_ref, queries_ref, key_ref, value_ref, keys_ref, values_ref = held
    for copy in copies[:-1]:
        copy.wait()
    positions = keys_ref.shape[1]
    mine = lax.axis_index("ctx")
    first = mine * positions
    core = lax.rem(mine, CORES)
    chip = (mine - core) // CORES
    groups = [
        jnp.bitwise_xor(chip, step) * CORES + which
        for which in (core, 1 - core)
        for step in (0, 3, 1, 2)
    ]
    heads = [pl.ds(pl.multiple_of(g * DH, DH), DH) for g in groups]
    scores = []
    for k in range(KVH):
        width = 8 * DH
        mine_q = queries_ref[:, pl.ds(pl.multiple_of(groups[k] * width, width), width)]
        mine_q = mine_q.astype(F32)
        query = jnp.concatenate([mine_q[:, h * DH : (h + 1) * DH] for h in range(8)], 0)
        if k == 0:
            own = jnp.sum(query * key_ref[...].astype(F32), -1, keepdims=True) * SCALE
        scores.append(
            lax.dot_general(
                query.astype(BF16),
                keys_ref[0, :, heads[k]],
                (((1,), (1,)), ((), ())),
                preferred_element_type=F32,
            )
        )
    score = jnp.concatenate(scores, 0) * SCALE
    place = first + lax.broadcasted_iota(jnp.int32, score.shape, 1)
    valid = place < lengths_ref[0]
    score = jnp.where(valid, score, LOW)
    own = jnp.concatenate([own, jnp.full((HQ - 8, 1), LOW, F32)], 0)
    peak = jnp.maximum(jnp.max(score, -1, keepdims=True), own)
    weight = jnp.where(valid, jnp.exp(score - peak), 0.0)
    own = jnp.exp(own[:8] - peak[:8])
    total = jnp.sum(weight, -1, keepdims=True)
    total = jnp.concatenate([total[:8] + own, total[8:]], 0)
    some = total > 0.0
    safe = jnp.where(some, total, 1.0)
    stats = spread(jnp.where(some, peak + jnp.log(safe), LOW))
    weight = weight.astype(BF16)
    copies[-1].wait()
    for k in range(KVH):
        rows = slice(k * 8, k * 8 + 8)
        numer = jnp.dot(weight[rows], values_ref[0, :, heads[k]], preferred_element_type=F32)
        if k == 0:
            numer = numer + own * value_ref[...].astype(F32)
        message = jnp.concatenate([numer / safe[rows], stats[rows]], 0).astype(BF16)
        out_ref = here_ref if k < KVH // CORES else there_ref
        out_ref[k % (KVH // CORES)] = message
    table = slots_ref[...]
    number = (
        lax.broadcasted_iota(jnp.int32, table.shape, 0) * table.shape[1]
        + lax.broadcasted_iota(jnp.int32, table.shape, 1)
    )
    me = lax.axis_index("span")
    idents = []
    for column in range(idents_ref.shape[0]):
        found = jnp.where(table == me * idents_ref.shape[0] + column, number, 0)
        found = jnp.sum(jnp.sum(found, 0, keepdims=True), 1, keepdims=True)
        idents.append(jnp.broadcast_to(found, (1, DH)))
    idents_ref[...] = jnp.concatenate(idents, 0).astype(F32)


def turn_kernel(keys_ref, out_ref):
    size = keys_ref.shape[2]
    for column in range(keys_ref.shape[0]):
        turned = keys_ref[column].astype(F32).T
        out_ref[column * size : (column + 1) * size, :] = turned.astype(BF16)


def span_kernel(gathered_ref, idents_ref, keys_ref, values_ref, out_ref):
    columns = values_ref.shape[0]
    requests = gathered_ref.shape[0]
    count = min(32, requests)
    rows = count * 8
    values = jnp.concatenate([values_ref[column] for column in range(columns)], 1)
    for start in range(0, requests, count):
        message = gathered_ref[start : start + count].astype(F32)
        query = message[:, :4].reshape(rows, DH)
        ids = message[:, 4, 0, :]
        code = jnp.zeros_like(ids)
        for column in range(columns):
            code = jnp.where(ids == idents_ref[column : column + 1, :], column + 1.0, code)
        code = jnp.max(code, -1, keepdims=True)
        code = jnp.broadcast_to(code[:, None, :], (count, 8, DH)).reshape(rows, DH)
        listed = [code == column + 1.0 for column in range(columns)]
        query = jnp.concatenate([jnp.where(here, query, 0.0) for here in listed], 1)
        score = jnp.dot(query.astype(BF16), keys_ref[...], preferred_element_type=F32)
        score = score * (SCALE * LOG2E)
        peak = jnp.max(score, -1, keepdims=True)
        weight = jnp.exp2(score - peak)
        total = jnp.sum(weight, -1, keepdims=True)
        lse = jnp.where(code[:, :1] > 0.0, peak * (1.0 / LOG2E) + jnp.log(total), LOW)
        numers = jnp.dot(weight.astype(BF16), values, preferred_element_type=F32)
        numer = jnp.zeros((rows, DH), F32)
        for column in range(columns):
            numer = jnp.where(listed[column], numers[:, column * DH : (column + 1) * DH], numer)
        attended = (numer / total).reshape(count, 8, DH)
        out_ref[start : start + count] = block_of(attended, lse.reshape(count, 8, 1))


def fold_kernel(first_ref, second_ref, *out_refs):
    parts = [first_ref[...].astype(F32), second_ref[...].astype(F32)]
    lses = [jnp.sum(part[:, 8:, :], -1, keepdims=True) for part in parts]
    peak = jnp.maximum(*lses)
    weights = [jnp.exp(lse - peak) for lse in lses]
    total = sum(weights)
    attended = sum(w * part[:, :8, :] for w, part in zip(weights, parts)) / total
    stats = spread(jnp.where(peak > LOW / 2, peak + jnp.log(total), LOW))
    result = jnp.concatenate([attended, stats], 1).astype(BF16)
    size = result.shape[0] // len(out_refs)
    for k, out_ref in enumerate(out_refs):
        out_ref[...] = result[k * size : (k + 1) * size]


def merge_kernel(spans_ref, here_ref, there_ref, out_ref):
    spans = spans_ref[...].astype(F32)
    attended = spans[:, :4].reshape(-1, 8, DH)
    row = jnp.broadcast_to(spans[:, 4, :1, :], attended.shape)
    kept = functools.reduce(jnp.logical_or, diagonals(attended.shape))
    lse = jnp.sum(jnp.where(kept, row, 0.0), -1, keepdims=True)
    tiles = [here_ref[0].astype(F32), there_ref[0].astype(F32)]
    lses = [jnp.sum(tile[8:], -1, keepdims=True) for tile in tiles]
    peak = functools.reduce(jnp.maximum, lses, jnp.max(lse, 0))
    weight = jnp.exp(lse - peak[None])
    weights = [jnp.exp(other - peak) for other in lses]
    total = sum(weights, jnp.sum(weight, 0))
    numer = sum(
        (w * tile[:8] for w, tile in zip(weights, tiles)), jnp.sum(weight * attended, 0)
    )
    result = numer / total
    out_ref[...] = jnp.concatenate([result[h : h + 1] for h in range(8)], 1).astype(BF16)


def vmem(count):
    return [pl.BlockSpec(memory_space=pltpu.VMEM)] * count


def hbm(count):
    return [pl.BlockSpec(memory_space=pltpu.HBM)] * count


def shards(
    queries,
    ctx_keys,
    ctx_values,
    lengths,
    new_key,
    new_value,
    span_keys,
    span_values,
    span_lists,
    span_slots,
):
    requests = lax.axis_size("span")
    chips = lax.axis_size("ctx") // CORES
    ch_dev = span_keys.shape[0]
    params = pltpu.CompilerParams(vmem_limit_bytes=16 * 1024 * 1024)
    alone = pltpu.CompilerParams(vmem_limit_bytes=56 * 1024 * 1024)
    blocks = jax.ShapeDtypeStruct((requests, 5, 2, DH), BF16)

    def tiles(count):
        return jax.ShapeDtypeStruct((count, 16, DH), BF16)

    def fold(here, there):
        return pl.pallas_call(
            fold_kernel,
            out_shape=[tiles(here.shape[0] // 2)] * 2,
            in_specs=vmem(2),
            out_specs=vmem(2),
            compiler_params=params,
            name="fold",
        )(here, there)

    packed = pl.pallas_call(
        pack_kernel,
        out_shape=blocks,
        in_specs=hbm(2),
        out_specs=hbm(1)[0],
        scratch_shapes=[
            pltpu.VMEM((requests // 4,) + blocks.shape[1:], BF16),
            pltpu.VMEM((1, KVH * DH), BF16),
            pltpu.VMEM(span_lists.shape, jnp.int32),
            pltpu.SemaphoreType.DMA((4,)),
        ],
        compiler_params=alone,
        name="pack",
    )(queries, span_lists)
    gathered = exchanged(packed)
    queries, span_keys, packed = lax.optimization_barrier((queries, span_keys, packed))
    table = span_slots.reshape(-1, min(DH, span_slots.shape[0]))
    fetched = (table, queries, new_key, new_value, ctx_keys, ctx_values)
    here, there, idents = pl.pallas_call(
        private_kernel,
        out_shape=[tiles(chips)] * CORES + [jax.ShapeDtypeStruct((ch_dev, DH), F32)],
        in_specs=hbm(1 + len(fetched)),
        out_specs=vmem(CORES + 1),
        scratch_shapes=[pltpu.SMEM(lengths.shape, jnp.int32)]
        + [pltpu.VMEM(array.shape, array.dtype) for array in fetched]
        + [pltpu.SemaphoreType.DMA((1 + len(fetched),))],
        compiler_params=alone,
        cost_estimate=pl.CostEstimate(
            flops=4 * HQ * ctx_keys.shape[1] * DH, bytes_accessed=1 << 20, transcendentals=1 << 14
        ),
        name="private",
    )(lengths, *fetched)
    there, gathered = lax.optimization_barrier((swapped(there, 1), gathered))
    turned = pl.pallas_call(
        turn_kernel,
        out_shape=jax.ShapeDtypeStruct((ch_dev * DH, span_keys.shape[1]), BF16),
        in_specs=vmem(1),
        out_specs=vmem(1)[0],
        compiler_params=params,
        name="turn",
    )(span_keys)
    partial = pl.pallas_call(
        span_kernel,
        out_shape=blocks,
        in_specs=vmem(4),
        out_specs=vmem(1)[0],
        compiler_params=params,
        cost_estimate=pl.CostEstimate(
            flops=4 * requests * 8 * DH * ch_dev * span_keys.shape[1],
            bytes_accessed=3 << 19,
            transcendentals=1 << 18,
        ),
        name="spans",
    )(gathered, idents, turned, span_values)
    partial = exchanged(partial)
    for mask in (1, 3):
        here, there = fold(here, there)
        there = swapped(there, mask * CORES)
    return pl.pallas_call(
        merge_kernel,
        out_shape=jax.ShapeDtypeStruct((1, KVH * DH), BF16),
        in_specs=vmem(3),
        out_specs=vmem(1)[0],
        compiler_params=params,
        name="merge",
    )(partial, here, there)


def solution(mesh):
    in_specs = (
        P("span", None),
        P("span", "ctx", None),
        P("span", "ctx", None),
        P("span"),
        P("span", "ctx"),
        P("span", "ctx"),
        P("span", None, "ctx"),
        P("span", None, "ctx"),
        P("span", None),
        P(),
    )
    out_specs = P("span", "ctx")
    return jax.shard_map(shards, mesh=mesh, in_specs=in_specs, out_specs=out_specs, check_vma=False)
```

```python
import functools

import jax
import jax.numpy as jnp
from jax import lax
from jax.experimental import pallas as pl
from jax.experimental.pallas import tpu as pltpu
from jax.sharding import PartitionSpec as P

HQ = 64
KVH = 8
DH = 128
CORES = 2
ROWS = 10
LOW = -1e30
SCALE = 1.0 / DH**0.5
F32 = jnp.float32
BF16 = jnp.bfloat16


def swapped(value, mask):
    n = lax.axis_size("ctx")
    return lax.ppermute(value, "ctx", [(i, i ^ mask) for i in range(n)])


def exchanged(value):
    n = lax.axis_size("span")
    first = n * 7 // 16
    order = [(first + k) % n for k in range(n)]
    blocks = value.reshape(n, ROWS // 2, 2, DH)
    blocks = lax.all_to_all(blocks, "span", 0, 0, axis_index_groups=[order], tiled=True)
    return blocks.reshape(value.shape)


def split(lse):
    high = lse.astype(BF16).astype(F32)
    rest = lse - high
    middle = rest.astype(BF16).astype(F32)
    return high, middle, rest - middle


def lanes(shape):
    return lax.broadcasted_iota(jnp.int32, shape, len(shape) - 1)


def spread(lse):
    lane = lanes(lse.shape[:-1] + (DH,))
    result = jnp.zeros(lane.shape, F32)
    for k, part in enumerate(split(lse)):
        result = jnp.where(lane == k, part, result)
    return result


def diagonal(count):
    shape = (count, 8, DH)
    return lanes(shape) == lax.broadcasted_iota(jnp.int32, shape, 1)


def heads_of(blocks, count):
    return jnp.concatenate(
        [blocks[k * ROWS : k * ROWS + 8] for k in range(count)], 0
    ).reshape(count, 8, DH)


def extras_of(blocks, count):
    return jnp.concatenate([blocks[k * ROWS + 8 : k * ROWS + 9] for k in range(count)], 0)


def fetch(pairs, sems):
    copies = [pltpu.make_async_copy(*pair, sems.at[k]) for k, pair in enumerate(pairs)]
    for copy in copies:
        copy.start()
    return copies


def pack_kernel(queries_ref, lists_ref, out_ref, held_ref, query_ref, ids_ref, sems):
    mine = lax.axis_index("ctx")
    width = KVH * DH
    part = queries_ref.at[:, pl.ds(pl.multiple_of(mine * width, width), width)]
    for copy in fetch(((part, query_ref), (lists_ref, ids_ref)), sems):
        copy.wait()
    query = query_ref[...].astype(F32)
    rows = [query[:, h * DH : (h + 1) * DH] for h in range(KVH)]
    ids = ids_ref[...].astype(F32)
    ids = jnp.concatenate([ids, jnp.full((1, DH - ids.shape[1]), -1.0, F32)], 1)
    count = held_ref.shape[0]
    held_ref[...] = jnp.concatenate((rows + [ids, ids]) * (count // ROWS), 0).astype(BF16)
    places = range(0, out_ref.shape[0], count)
    pairs = [(held_ref, out_ref.at[pl.ds(place, count)]) for place in places]
    for copy in fetch(pairs, sems):
        copy.wait()


def private_kernel(*refs):
    count = len(refs) // 2 - 2
    here_ref, there_ref, idents_ref = refs[count : count + 3]
    held, sems = refs[count + 3 : -1], refs[-1]
    copies = fetch(tuple(zip(refs[:count], held)), sems)
    lengths_ref, slots_ref, queries_ref, key_ref, value_ref, keys_ref, values_ref = held
    for copy in copies[:-1]:
        copy.wait()
    positions = keys_ref.shape[1]
    mine = lax.axis_index("ctx")
    first = mine * positions
    core = lax.rem(mine, CORES)
    chip = (mine - core) // CORES
    groups = [
        jnp.bitwise_xor(chip, step) * CORES + which
        for step in (0, 3, 1, 2)
        for which in (core, 1 - core)
    ]
    heads = [pl.ds(pl.multiple_of(g * DH, DH), DH) for g in groups]
    scores = []
    for k in range(KVH):
        width = 8 * DH
        mine_q = queries_ref[:, pl.ds(pl.multiple_of(groups[k] * width, width), width)]
        mine_q = mine_q.astype(F32)
        query = jnp.concatenate([mine_q[:, h * DH : (h + 1) * DH] for h in range(8)], 0)
        if k == 0:
            own = jnp.sum(query * key_ref[...].astype(F32), -1, keepdims=True) * SCALE
        scores.append(
            lax.dot_general(
                query.astype(BF16),
                keys_ref[0, :, heads[k]],
                (((1,), (1,)), ((), ())),
                preferred_element_type=F32,
            )
        )
    score = jnp.concatenate(scores, 0) * SCALE
    place = first + lax.broadcasted_iota(jnp.int32, score.shape, 1)
    valid = place < lengths_ref[0]
    score = jnp.where(valid, score, LOW)
    own = jnp.concatenate([own, jnp.full((HQ - 8, 1), LOW, F32)], 0)
    peak = jnp.maximum(jnp.max(score, -1, keepdims=True), own)
    weight = jnp.where(valid, jnp.exp(score - peak), 0.0)
    own = jnp.exp(own[:8] - peak[:8])
    total = jnp.sum(weight, -1, keepdims=True)
    total = jnp.concatenate([total[:8] + own, total[8:]], 0)
    some = total > 0.0
    safe = jnp.where(some, total, 1.0)
    stats = spread(jnp.where(some, peak + jnp.log(safe), LOW))
    weight = weight.astype(BF16)
    copies[-1].wait()
    for k in range(KVH):
        rows = slice(k * 8, k * 8 + 8)
        numer = jnp.dot(weight[rows], values_ref[0, :, heads[k]], preferred_element_type=F32)
        if k == 0:
            numer = numer + own * value_ref[...].astype(F32)
        message = jnp.concatenate([numer / safe[rows], stats[rows]], 0).astype(BF16)
        out_ref = here_ref if k < KVH // 2 else there_ref
        out_ref[k % (KVH // 2)] = message
    table = slots_ref[...]
    number = (
        lax.broadcasted_iota(jnp.int32, table.shape, 0) * table.shape[1]
        + lax.broadcasted_iota(jnp.int32, table.shape, 1)
    )
    me = lax.axis_index("span")
    idents = []
    for column in range(idents_ref.shape[0]):
        found = jnp.where(table == me * idents_ref.shape[0] + column, number, 0)
        found = jnp.sum(jnp.sum(found, 0, keepdims=True), 1, keepdims=True)
        idents.append(jnp.broadcast_to(found, (1, DH)))
    idents_ref[...] = jnp.concatenate(idents, 0).astype(F32)


def span_kernel(gathered_ref, idents_ref, keys_ref, values_ref, out_ref, held_ref):
    columns = keys_ref.shape[0]
    requests = gathered_ref.shape[0] // ROWS
    count = requests // 2
    rows = count * 8
    keys = jnp.concatenate([keys_ref[column] for column in range(columns)], 1)
    values = jnp.concatenate([values_ref[column] for column in range(columns)], 1)
    for start in range(0, requests, count):
        part = slice(start * ROWS, (start + count) * ROWS)
        message = gathered_ref[part].astype(F32)
        query = heads_of(message, count).reshape(rows, DH)
        ids = extras_of(message, count)
        code = jnp.zeros_like(ids)
        for column in range(columns):
            code = jnp.where(ids == idents_ref[column : column + 1, :], column + 1.0, code)
        code = jnp.max(code, -1, keepdims=True)
        code = jnp.broadcast_to(code[:, None, :], (count, 8, DH)).reshape(rows, DH)
        listed = [code == column + 1.0 for column in range(columns)]
        query = jnp.concatenate([jnp.where(here, query, 0.0) for here in listed], 1)
        score = SCALE * lax.dot_general(
            query.astype(BF16), keys, (((1,), (1,)), ((), ())), preferred_element_type=F32
        )
        peak = jnp.max(score, -1, keepdims=True)
        weight = jnp.exp(score - peak)
        total = jnp.sum(weight, -1, keepdims=True)
        lse = jnp.where(code[:, :1] > 0.0, peak + jnp.log(total), LOW)
        numers = jnp.dot(weight.astype(BF16), values, preferred_element_type=F32)
        numer = jnp.zeros((rows, DH), F32)
        for column in range(columns):
            numer = jnp.where(listed[column], numers[:, column * DH : (column + 1) * DH], numer)
        attended = numer / total
        lse = jnp.where(diagonal(count), lse.reshape(count, 8, 1), 0.0)
        high, middle, last = split(jnp.sum(lse, 1))
        extras = high + pltpu.roll(middle, 8, 1) + pltpu.roll(last, 16, 1)
        for k in range(count):
            held_ref[k * ROWS : k * ROWS + 8] = attended[k * 8 : k * 8 + 8]
            held_ref[k * ROWS + 8 : k * ROWS + ROWS] = jnp.broadcast_to(extras[k : k + 1], (2, DH))
        out_ref[part] = held_ref[...].astype(BF16)


def fold_kernel(first_ref, second_ref, *out_refs):
    parts = [first_ref[...].astype(F32), second_ref[...].astype(F32)]
    lses = [jnp.sum(part[:, 8:, :], -1, keepdims=True) for part in parts]
    peak = jnp.maximum(*lses)
    weights = [jnp.exp(lse - peak) for lse in lses]
    total = sum(weights)
    attended = sum(w * part[:, :8, :] for w, part in zip(weights, parts)) / total
    stats = spread(jnp.where(peak > LOW / 2, peak + jnp.log(total), LOW))
    result = jnp.concatenate([attended, stats], 1).astype(BF16)
    size = result.shape[0] // len(out_refs)
    for k, out_ref in enumerate(out_refs):
        out_ref[...] = result[k * size : (k + 1) * size]


def merge_kernel(spans_ref, here_ref, there_ref, out_ref):
    count = spans_ref.shape[0] // ROWS
    spans = spans_ref[...].astype(F32)
    tiles = [here_ref[0].astype(F32), there_ref[0].astype(F32)]
    attended = [tile[:8] for tile in tiles] + [heads_of(spans, count)]
    parts = extras_of(spans, count)
    lses = [
        jnp.sum(jnp.where(diagonal(1)[0], jnp.sum(tile[8:], -1, keepdims=True), 0.0), 0)[None]
        for tile in tiles
    ] + [parts + pltpu.roll(parts, DH - 8, 1) + pltpu.roll(parts, DH - 16, 1)]
    peak = functools.reduce(jnp.maximum, [jnp.max(lse, 0, keepdims=True) for lse in lses])
    weights = [jnp.exp(lse - peak) for lse in lses]
    scale = 1.0 / sum(jnp.sum(weight, 0, keepdims=True) for weight in weights)
    result = jnp.zeros((8, DH), F32)
    for weight, values in zip(weights, attended):
        weight = (weight * scale)[:, None, :]
        weight = jnp.sum(jnp.where(diagonal(weight.shape[0]), weight, 0.0), -1, keepdims=True)
        result = result + jnp.sum(weight * values, 0)
    out_ref[...] = jnp.concatenate([result[h : h + 1] for h in range(8)], 1).astype(BF16)


def vmem(count):
    return [pl.BlockSpec(memory_space=pltpu.VMEM)] * count


def hbm(count):
    return [pl.BlockSpec(memory_space=pltpu.HBM)] * count


def shards(
    queries,
    ctx_keys,
    ctx_values,
    lengths,
    new_key,
    new_value,
    span_keys,
    span_values,
    span_lists,
    span_slots,
):
    requests = lax.axis_size("span")
    ch_dev = span_keys.shape[0]
    params = pltpu.CompilerParams(vmem_limit_bytes=16 * 1024 * 1024)
    alone = pltpu.CompilerParams(vmem_limit_bytes=56 * 1024 * 1024)
    blocks = jax.ShapeDtypeStruct((requests * ROWS, DH), BF16)

    def tiles(count):
        return jax.ShapeDtypeStruct((count, 16, DH), BF16)

    def fold(here, there):
        return pl.pallas_call(
            fold_kernel,
            out_shape=[tiles(here.shape[0] // 2)] * 2,
            in_specs=vmem(2),
            out_specs=vmem(2),
            compiler_params=params,
            name="fold",
        )(here, there)

    packed = pl.pallas_call(
        pack_kernel,
        out_shape=blocks,
        in_specs=hbm(2),
        out_specs=hbm(1)[0],
        scratch_shapes=[
            pltpu.VMEM((blocks.shape[0] // 4, DH), BF16),
            pltpu.VMEM((1, KVH * DH), BF16),
            pltpu.VMEM(span_lists.shape, jnp.int32),
            pltpu.SemaphoreType.DMA((4,)),
        ],
        compiler_params=alone,
        name="pack",
    )(queries, span_lists)
    gathered = exchanged(packed)
    queries, packed = lax.optimization_barrier((queries, packed))
    table = span_slots.reshape(-1, min(DH, span_slots.shape[0]))
    fetched = (table, queries, new_key, new_value, ctx_keys, ctx_values)
    here, there, idents = pl.pallas_call(
        private_kernel,
        out_shape=[tiles(KVH // 2)] * 2 + [jax.ShapeDtypeStruct((ch_dev, DH), F32)],
        in_specs=hbm(1 + len(fetched)),
        out_specs=vmem(3),
        scratch_shapes=[pltpu.SMEM(lengths.shape, jnp.int32)]
        + [pltpu.VMEM(array.shape, array.dtype) for array in fetched]
        + [pltpu.SemaphoreType.DMA((1 + len(fetched),))],
        compiler_params=alone,
        cost_estimate=pl.CostEstimate(
            flops=4 * HQ * ctx_keys.shape[1] * DH, bytes_accessed=1 << 20, transcendentals=1 << 14
        ),
        name="private",
    )(lengths, *fetched)
    there, gathered = lax.optimization_barrier((swapped(there, CORES), gathered))
    partial = pl.pallas_call(
        span_kernel,
        out_shape=blocks,
        in_specs=vmem(4),
        out_specs=vmem(1)[0],
        scratch_shapes=[pltpu.VMEM((blocks.shape[0] // 2, DH), F32)],
        compiler_params=params,
        cost_estimate=pl.CostEstimate(
            flops=4 * requests * 8 * DH * ch_dev * span_keys.shape[1],
            bytes_accessed=3 << 19,
            transcendentals=1 << 18,
        ),
        name="spans",
    )(gathered, idents, span_keys, span_values)
    partial = exchanged(partial)
    for mask in (3 * CORES, 1):
        here, there = fold(here, there)
        there = swapped(there, mask)
    return pl.pallas_call(
        merge_kernel,
        out_shape=jax.ShapeDtypeStruct((1, KVH * DH), BF16),
        in_specs=vmem(3),
        out_specs=vmem(1)[0],
        compiler_params=params,
        name="merge",
    )(partial, here, there)


def solution(mesh):
    in_specs = (
        P("span", None),
        P("span", "ctx", None),
        P("span", "ctx", None),
        P("span"),
        P("span", "ctx"),
        P("span", "ctx"),
        P("span", None, "ctx"),
        P("span", None, "ctx"),
        P("span", None),
        P(),
    )
    out_specs = P("span", "ctx")
    return jax.shard_map(shards, mesh=mesh, in_specs=in_specs, out_specs=out_specs, check_vma=False)
```

```python
import functools

import jax
import jax.numpy as jnp
from jax import lax
from jax.experimental import pallas as pl
from jax.experimental.pallas import tpu as pltpu
from jax.sharding import PartitionSpec as P

HQ = 64
KVH = 8
DH = 128
CORES = 2
ROWS = 10
LOW = -1e30
SCALE = 1.0 / DH**0.5
F32 = jnp.float32
BF16 = jnp.bfloat16


def swapped(value, mask):
    n = lax.axis_size("ctx")
    return lax.ppermute(value, "ctx", [(i, i ^ mask) for i in range(n)])


def firsts():
    n = lax.axis_size("span")
    return n * 7 // 16, n * 29 // 64


def exchanged(value, first):
    n = lax.axis_size("span")
    order = [(first + k) % n for k in range(n)]
    blocks = value.reshape(n, ROWS // 2, 2, DH)
    blocks = lax.all_to_all(blocks, "span", 0, 0, axis_index_groups=[order], tiled=True)
    return blocks.reshape(value.shape)


def split(lse):
    high = lse.astype(BF16).astype(F32)
    rest = lse - high
    middle = rest.astype(BF16).astype(F32)
    return high, middle, rest - middle


def lanes(shape):
    return lax.broadcasted_iota(jnp.int32, shape, len(shape) - 1)


def spread(lse):
    lane = lanes(lse.shape[:-1] + (DH,))
    result = jnp.zeros(lane.shape, F32)
    for k, part in enumerate(split(lse)):
        result = jnp.where(lane == k, part, result)
    return result


def diagonal(count):
    shape = (count, 8, DH)
    return lanes(shape) == lax.broadcasted_iota(jnp.int32, shape, 1)


def heads_of(blocks, count):
    return jnp.concatenate(
        [blocks[k * ROWS : k * ROWS + 8] for k in range(count)], 0
    ).reshape(count, 8, DH)


def extras_of(blocks, count):
    return jnp.concatenate([blocks[k * ROWS + 8 : k * ROWS + 9] for k in range(count)], 0)


def fetch(pairs, sems):
    copies = [pltpu.make_async_copy(*pair, sems.at[k]) for k, pair in enumerate(pairs)]
    for copy in copies:
        copy.start()
    return copies


def pack_kernel(queries_ref, lists_ref, out_ref, held_ref, query_ref, ids_ref, sems):
    mine = lax.axis_index("ctx")
    width = KVH * DH
    part = queries_ref.at[:, pl.ds(pl.multiple_of(mine * width, width), width)]
    for copy in fetch(((part, query_ref), (lists_ref, ids_ref)), sems):
        copy.wait()
    query = query_ref[...].astype(F32)
    rows = [query[:, h * DH : (h + 1) * DH] for h in range(KVH)]
    ids = ids_ref[...].astype(F32)
    ids = jnp.concatenate([ids, jnp.full((1, DH - ids.shape[1]), -1.0, F32)], 1)
    count = held_ref.shape[0]
    held_ref[...] = jnp.concatenate((rows + [ids, ids]) * (count // ROWS), 0).astype(BF16)
    places = range(0, out_ref.shape[0], count)
    pairs = [(held_ref, out_ref.at[pl.ds(place, count)]) for place in places]
    for copy in fetch(pairs, sems):
        copy.wait()


def private_kernel(*refs):
    count = len(refs) // 2 - 2
    here_ref, there_ref, idents_ref = refs[count : count + 3]
    held, sems = refs[count + 3 : -1], refs[-1]
    copies = fetch(tuple(zip(refs[:count], held)), sems)
    lengths_ref, slots_ref, queries_ref, key_ref, value_ref, keys_ref, values_ref = held
    for copy in copies[:-1]:
        copy.wait()
    positions = keys_ref.shape[1]
    mine = lax.axis_index("ctx")
    first = mine * positions
    core = lax.rem(mine, CORES)
    chip = (mine - core) // CORES
    groups = [
        jnp.bitwise_xor(chip, step) * CORES + which
        for which in (core, 1 - core)
        for step in (0, 3, 1, 2)
    ]
    heads = [pl.ds(pl.multiple_of(g * DH, DH), DH) for g in groups]
    scores = []
    for k in range(KVH):
        width = 8 * DH
        mine_q = queries_ref[:, pl.ds(pl.multiple_of(groups[k] * width, width), width)]
        mine_q = mine_q.astype(F32)
        query = jnp.concatenate([mine_q[:, h * DH : (h + 1) * DH] for h in range(8)], 0)
        if k == 0:
            own = jnp.sum(query * key_ref[...].astype(F32), -1, keepdims=True) * SCALE
        scores.append(
            lax.dot_general(
                query.astype(BF16),
                keys_ref[0, :, heads[k]],
                (((1,), (1,)), ((), ())),
                preferred_element_type=F32,
            )
        )
    score = jnp.concatenate(scores, 0) * SCALE
    place = first + lax.broadcasted_iota(jnp.int32, score.shape, 1)
    valid = place < lengths_ref[0]
    score = jnp.where(valid, score, LOW)
    own = jnp.concatenate([own, jnp.full((HQ - 8, 1), LOW, F32)], 0)
    peak = jnp.maximum(jnp.max(score, -1, keepdims=True), own)
    weight = jnp.where(valid, jnp.exp(score - peak), 0.0)
    own = jnp.exp(own[:8] - peak[:8])
    total = jnp.sum(weight, -1, keepdims=True)
    total = jnp.concatenate([total[:8] + own, total[8:]], 0)
    some = total > 0.0
    safe = jnp.where(some, total, 1.0)
    stats = spread(jnp.where(some, peak + jnp.log(safe), LOW))
    weight = weight.astype(BF16)
    copies[-1].wait()
    for k in range(KVH):
        rows = slice(k * 8, k * 8 + 8)
        numer = jnp.dot(weight[rows], values_ref[0, :, heads[k]], preferred_element_type=F32)
        if k == 0:
            numer = numer + own * value_ref[...].astype(F32)
        message = jnp.concatenate([numer / safe[rows], stats[rows]], 0).astype(BF16)
        out_ref = here_ref if k < KVH // CORES else there_ref
        out_ref[k % (KVH // CORES)] = message
    table = slots_ref[...]
    number = (
        lax.broadcasted_iota(jnp.int32, table.shape, 0) * table.shape[1]
        + lax.broadcasted_iota(jnp.int32, table.shape, 1)
    )
    me = lax.axis_index("span")
    idents = []
    for column in range(idents_ref.shape[0]):
        found = jnp.where(table == me * idents_ref.shape[0] + column, number, 0)
        found = jnp.sum(jnp.sum(found, 0, keepdims=True), 1, keepdims=True)
        idents.append(jnp.broadcast_to(found, (1, DH)))
    idents_ref[...] = jnp.concatenate(idents, 0).astype(F32)


def span_kernel(gathered_ref, idents_ref, keys_ref, values_ref, out_ref, held_ref):
    columns = keys_ref.shape[0]
    requests = gathered_ref.shape[0] // ROWS
    count = requests // 2
    there, back = firsts()
    rows = count * 8
    keys = jnp.concatenate([keys_ref[column] for column in range(columns)], 1)
    values = jnp.concatenate([values_ref[column] for column in range(columns)], 1)
    for start in range(0, requests, count):
        part = slice(start * ROWS, (start + count) * ROWS)
        message = gathered_ref[part].astype(F32)
        query = heads_of(message, count).reshape(rows, DH)
        ids = extras_of(message, count)
        code = jnp.zeros_like(ids)
        for column in range(columns):
            code = jnp.where(ids == idents_ref[column : column + 1, :], column + 1.0, code)
        code = jnp.max(code, -1, keepdims=True)
        code = jnp.broadcast_to(code[:, None, :], (count, 8, DH)).reshape(rows, DH)
        listed = [code == column + 1.0 for column in range(columns)]
        query = jnp.concatenate([jnp.where(here, query, 0.0) for here in listed], 1)
        score = SCALE * lax.dot_general(
            query.astype(BF16), keys, (((1,), (1,)), ((), ())), preferred_element_type=F32
        )
        peak = jnp.max(score, -1, keepdims=True)
        weight = jnp.exp(score - peak)
        total = jnp.sum(weight, -1, keepdims=True)
        lse = jnp.where(code[:, :1] > 0.0, peak + jnp.log(total), LOW)
        numers = jnp.dot(weight.astype(BF16), values, preferred_element_type=F32)
        numer = jnp.zeros((rows, DH), F32)
        for column in range(columns):
            numer = jnp.where(listed[column], numers[:, column * DH : (column + 1) * DH], numer)
        attended = numer / total
        lse = jnp.where(diagonal(count), lse.reshape(count, 8, 1), 0.0)
        high, middle, last = split(jnp.sum(lse, 1))
        extras = high + pltpu.roll(middle, 8, 1) + pltpu.roll(last, 16, 1)
        for k in range(count):
            row = (start + k + there - back) % requests * ROWS
            held_ref[row : row + 8] = attended[k * 8 : k * 8 + 8]
            held_ref[row + 8 : row + ROWS] = jnp.broadcast_to(extras[k : k + 1], (2, DH))
    out_ref[...] = held_ref[...].astype(BF16)


def fold_kernel(first_ref, second_ref, *out_refs):
    parts = [first_ref[...].astype(F32), second_ref[...].astype(F32)]
    lses = [jnp.sum(part[:, 8:, :], -1, keepdims=True) for part in parts]
    peak = jnp.maximum(*lses)
    weights = [jnp.exp(lse - peak) for lse in lses]
    total = sum(weights)
    attended = sum(w * part[:, :8, :] for w, part in zip(weights, parts)) / total
    stats = spread(jnp.where(peak > LOW / 2, peak + jnp.log(total), LOW))
    result = jnp.concatenate([attended, stats], 1).astype(BF16)
    size = result.shape[0] // len(out_refs)
    for k, out_ref in enumerate(out_refs):
        out_ref[...] = result[k * size : (k + 1) * size]


def merge_kernel(spans_ref, here_ref, there_ref, out_ref):
    count = spans_ref.shape[0] // ROWS
    spans = spans_ref[...].astype(F32)
    tiles = [here_ref[0].astype(F32), there_ref[0].astype(F32)]
    attended = [tile[:8] for tile in tiles] + [heads_of(spans, count)]
    parts = extras_of(spans, count)
    lses = [
        jnp.sum(jnp.where(diagonal(1)[0], jnp.sum(tile[8:], -1, keepdims=True), 0.0), 0)[None]
        for tile in tiles
    ] + [parts + pltpu.roll(parts, DH - 8, 1) + pltpu.roll(parts, DH - 16, 1)]
    peak = functools.reduce(jnp.maximum, [jnp.max(lse, 0, keepdims=True) for lse in lses])
    weights = [jnp.exp(lse - peak) for lse in lses]
    scale = 1.0 / sum(jnp.sum(weight, 0, keepdims=True) for weight in weights)
    result = jnp.zeros((8, DH), F32)
    for weight, values in zip(weights, attended):
        weight = (weight * scale)[:, None, :]
        weight = jnp.sum(jnp.where(diagonal(weight.shape[0]), weight, 0.0), -1, keepdims=True)
        result = result + jnp.sum(weight * values, 0)
    out_ref[...] = jnp.concatenate([result[h : h + 1] for h in range(8)], 1).astype(BF16)


def vmem(count):
    return [pl.BlockSpec(memory_space=pltpu.VMEM)] * count


def hbm(count):
    return [pl.BlockSpec(memory_space=pltpu.HBM)] * count


def shards(
    queries,
    ctx_keys,
    ctx_values,
    lengths,
    new_key,
    new_value,
    span_keys,
    span_values,
    span_lists,
    span_slots,
):
    requests = lax.axis_size("span")
    chips = lax.axis_size("ctx") // CORES
    ch_dev = span_keys.shape[0]
    params = pltpu.CompilerParams(vmem_limit_bytes=16 * 1024 * 1024)
    alone = pltpu.CompilerParams(vmem_limit_bytes=56 * 1024 * 1024)
    blocks = jax.ShapeDtypeStruct((requests * ROWS, DH), BF16)

    def tiles(count):
        return jax.ShapeDtypeStruct((count, 16, DH), BF16)

    def fold(here, there):
        return pl.pallas_call(
            fold_kernel,
            out_shape=[tiles(here.shape[0] // 2)] * 2,
            in_specs=vmem(2),
            out_specs=vmem(2),
            compiler_params=params,
            name="fold",
        )(here, there)

    packed = pl.pallas_call(
        pack_kernel,
        out_shape=blocks,
        in_specs=hbm(2),
        out_specs=hbm(1)[0],
        scratch_shapes=[
            pltpu.VMEM((blocks.shape[0] // 4, DH), BF16),
            pltpu.VMEM((1, KVH * DH), BF16),
            pltpu.VMEM(span_lists.shape, jnp.int32),
            pltpu.SemaphoreType.DMA((4,)),
        ],
        compiler_params=alone,
        name="pack",
    )(queries, span_lists)
    gathered = exchanged(packed, firsts()[0])
    queries, packed = lax.optimization_barrier((queries, packed))
    table = span_slots.reshape(-1, min(DH, span_slots.shape[0]))
    fetched = (table, queries, new_key, new_value, ctx_keys, ctx_values)
    here, there, idents = pl.pallas_call(
        private_kernel,
        out_shape=[tiles(chips)] * CORES + [jax.ShapeDtypeStruct((ch_dev, DH), F32)],
        in_specs=hbm(1 + len(fetched)),
        out_specs=vmem(CORES + 1),
        scratch_shapes=[pltpu.SMEM(lengths.shape, jnp.int32)]
        + [pltpu.VMEM(array.shape, array.dtype) for array in fetched]
        + [pltpu.SemaphoreType.DMA((1 + len(fetched),))],
        compiler_params=alone,
        cost_estimate=pl.CostEstimate(
            flops=4 * HQ * ctx_keys.shape[1] * DH, bytes_accessed=1 << 20, transcendentals=1 << 14
        ),
        name="private",
    )(lengths, *fetched)
    there, gathered = lax.optimization_barrier((swapped(there, 1), gathered))
    partial = pl.pallas_call(
        span_kernel,
        out_shape=blocks,
        in_specs=vmem(4),
        out_specs=vmem(1)[0],
        scratch_shapes=[pltpu.VMEM(blocks.shape, F32)],
        compiler_params=params,
        cost_estimate=pl.CostEstimate(
            flops=4 * requests * 8 * DH * ch_dev * span_keys.shape[1],
            bytes_accessed=3 << 19,
            transcendentals=1 << 18,
        ),
        name="spans",
    )(gathered, idents, span_keys, span_values)
    partial = exchanged(partial, firsts()[1])
    for mask in (1, 3):
        here, there = fold(here, there)
        there = swapped(there, mask * CORES)
    return pl.pallas_call(
        merge_kernel,
        out_shape=jax.ShapeDtypeStruct((1, KVH * DH), BF16),
        in_specs=vmem(3),
        out_specs=vmem(1)[0],
        compiler_params=params,
        name="merge",
    )(partial, here, there)


def solution(mesh):
    in_specs = (
        P("span", None),
        P("span", "ctx", None),
        P("span", "ctx", None),
        P("span"),
        P("span", "ctx"),
        P("span", "ctx"),
        P("span", None, "ctx"),
        P("span", None, "ctx"),
        P("span", None),
        P(),
    )
    out_specs = P("span", "ctx")
    return jax.shard_map(shards, mesh=mesh, in_specs=in_specs, out_specs=out_specs, check_vma=False)
```

```python
import functools

import jax
import jax.numpy as jnp
from jax import lax
from jax.experimental import pallas as pl
from jax.experimental.pallas import tpu as pltpu
from jax.sharding import PartitionSpec as P

HQ = 64
KVH = 8
DH = 128
CORES = 2
LOW = -1e30
SCALE = 1.0 / DH**0.5
LOG2E = 1.4426950408889634
F32 = jnp.float32
BF16 = jnp.bfloat16


def swapped(value, mask):
    n = lax.axis_size("ctx")
    return lax.ppermute(value, "ctx", [(i, i ^ mask) for i in range(n)])


def exchanged(value):
    n = lax.axis_size("span")
    first = n * 29 // 64
    order = [(first + k) % n for k in range(n)]
    return lax.all_to_all(value, "span", 0, 0, axis_index_groups=[order], tiled=True)


def split(lse):
    high = lse.astype(BF16).astype(F32)
    rest = lse - high
    middle = rest.astype(BF16).astype(F32)
    return high, middle, rest - middle


def lanes(shape):
    return lax.broadcasted_iota(jnp.int32, shape, len(shape) - 1)


def spread(lse):
    lane = lanes(lse.shape[:-1] + (DH,))
    result = jnp.zeros(lane.shape, F32)
    for k, part in enumerate(split(lse)):
        result = jnp.where(lane == k, part, result)
    return result


def diagonals(shape):
    head = lax.broadcasted_iota(jnp.int32, shape, 1)
    return [lanes(shape) == head + 8 * k for k in range(3)]


def block_of(attended, lse):
    count = attended.shape[0]
    row = jnp.zeros(attended.shape, F32)
    for where, part in zip(diagonals(attended.shape), split(lse)):
        row = jnp.where(where, part, row)
    row = jnp.sum(row, 1, keepdims=True)
    row = jnp.broadcast_to(row, (count, 2, DH)).reshape(count, 1, 2, DH)
    return jnp.concatenate([attended.reshape(count, 4, 2, DH), row], 1).astype(BF16)


def fetch(pairs, sems):
    copies = [pltpu.make_async_copy(*pair, sems.at[k]) for k, pair in enumerate(pairs)]
    for copy in copies:
        copy.start()
    return copies


def pack_kernel(queries_ref, lists_ref, out_ref, held_ref, query_ref, ids_ref, sems):
    mine = lax.axis_index("ctx")
    width = KVH * DH
    part = queries_ref.at[:, pl.ds(pl.multiple_of(mine * width, width), width)]
    for copy in fetch(((part, query_ref), (lists_ref, ids_ref)), sems):
        copy.wait()
    query = query_ref[...].astype(F32)
    rows = [query[:, h * DH : (h + 1) * DH] for h in range(KVH)]
    ids = ids_ref[...].astype(F32)
    ids = jnp.concatenate([ids, jnp.full((1, DH - ids.shape[1]), -1.0, F32)], 1)
    block = jnp.concatenate(rows + [ids, ids], 0).reshape(5, 2, DH).astype(BF16)
    count = held_ref.shape[0]
    for copy in range(count):
        held_ref[copy] = block
    places = range(0, out_ref.shape[0], count)
    pairs = [(held_ref, out_ref.at[pl.ds(place, count)]) for place in places]
    for copy in fetch(pairs, sems):
        copy.wait()


def private_kernel(*refs):
    count = len(refs) // 2 - 2
    here_ref, there_ref, idents_ref = refs[count : count + 3]
    held, sems = refs[count + 3 : -1], refs[-1]
    copies = fetch(tuple(zip(refs[:count], held)), sems)
    lengths_ref, slots_ref, queries_ref, key_ref, value_ref, keys_ref, values_ref = held
    for copy in copies[:-1]:
        copy.wait()
    positions = keys_ref.shape[1]
    mine = lax.axis_index("ctx")
    first = mine * positions
    core = lax.rem(mine, CORES)
    chip = (mine - core) // CORES
    groups = [
        jnp.bitwise_xor(chip, step) * CORES + which
        for which in (core, 1 - core)
        for step in (0, 3, 1, 2)
    ]
    heads = [pl.ds(pl.multiple_of(g * DH, DH), DH) for g in groups]
    scores = []
    for k in range(KVH):
        width = 8 * DH
        mine_q = queries_ref[:, pl.ds(pl.multiple_of(groups[k] * width, width), width)]
        mine_q = mine_q.astype(F32)
        query = jnp.concatenate([mine_q[:, h * DH : (h + 1) * DH] for h in range(8)], 0)
        if k == 0:
            own = jnp.sum(query * key_ref[...].astype(F32), -1, keepdims=True) * SCALE
        scores.append(
            lax.dot_general(
                query.astype(BF16),
                keys_ref[0, :, heads[k]],
                (((1,), (1,)), ((), ())),
                preferred_element_type=F32,
            )
        )
    score = jnp.concatenate(scores, 0) * SCALE
    place = first + lax.broadcasted_iota(jnp.int32, score.shape, 1)
    valid = place < lengths_ref[0]
    score = jnp.where(valid, score, LOW)
    own = jnp.concatenate([own, jnp.full((HQ - 8, 1), LOW, F32)], 0)
    peak = jnp.maximum(jnp.max(score, -1, keepdims=True), own)
    weight = jnp.where(valid, jnp.exp(score - peak), 0.0)
    own = jnp.exp(own[:8] - peak[:8])
    total = jnp.sum(weight, -1, keepdims=True)
    total = jnp.concatenate([total[:8] + own, total[8:]], 0)
    some = total > 0.0
    safe = jnp.where(some, total, 1.0)
    stats = spread(jnp.where(some, peak + jnp.log(safe), LOW))
    weight = weight.astype(BF16)
    copies[-1].wait()
    for k in range(KVH):
        rows = slice(k * 8, k * 8 + 8)
        numer = jnp.dot(weight[rows], values_ref[0, :, heads[k]], preferred_element_type=F32)
        if k == 0:
            numer = numer + own * value_ref[...].astype(F32)
        message = jnp.concatenate([numer / safe[rows], stats[rows]], 0).astype(BF16)
        out_ref = here_ref if k < KVH // CORES else there_ref
        out_ref[k % (KVH // CORES)] = message
    table = slots_ref[...]
    number = (
        lax.broadcasted_iota(jnp.int32, table.shape, 0) * table.shape[1]
        + lax.broadcasted_iota(jnp.int32, table.shape, 1)
    )
    me = lax.axis_index("span")
    idents = []
    for column in range(idents_ref.shape[0]):
        found = jnp.where(table == me * idents_ref.shape[0] + column, number, 0)
        found = jnp.sum(jnp.sum(found, 0, keepdims=True), 1, keepdims=True)
        idents.append(jnp.broadcast_to(found, (1, DH)))
    idents_ref[...] = jnp.concatenate(idents, 0).astype(F32)


def turn_kernel(keys_ref, out_ref):
    size = keys_ref.shape[2]
    for column in range(keys_ref.shape[0]):
        turned = keys_ref[column].astype(F32).T
        out_ref[column * size : (column + 1) * size, :] = turned.astype(BF16)


def span_kernel(gathered_ref, idents_ref, keys_ref, values_ref, out_ref):
    columns = values_ref.shape[0]
    requests = gathered_ref.shape[0]
    count = min(32, requests)
    rows = count * 8
    values = jnp.concatenate([values_ref[column] for column in range(columns)], 1)
    for start in range(0, requests, count):
        message = gathered_ref[start : start + count].astype(F32)
        query = message[:, :4].reshape(rows, DH)
        ids = message[:, 4, 0, :]
        code = jnp.zeros_like(ids)
        for column in range(columns):
            code = jnp.where(ids == idents_ref[column : column + 1, :], column + 1.0, code)
        code = jnp.max(code, -1, keepdims=True)
        code = jnp.broadcast_to(code[:, None, :], (count, 8, DH)).reshape(rows, DH)
        listed = [code == column + 1.0 for column in range(columns)]
        query = jnp.concatenate([jnp.where(here, query, 0.0) for here in listed], 1)
        score = jnp.dot(query.astype(BF16), keys_ref[...], preferred_element_type=F32)
        score = score * (SCALE * LOG2E)
        peak = jnp.max(score, -1, keepdims=True)
        weight = jnp.exp2(score - peak)
        total = jnp.sum(weight, -1, keepdims=True)
        lse = jnp.where(code[:, :1] > 0.0, peak * (1.0 / LOG2E) + jnp.log(total), LOW)
        numers = jnp.dot(weight.astype(BF16), values, preferred_element_type=F32)
        numer = jnp.zeros((rows, DH), F32)
        for column in range(columns):
            numer = jnp.where(listed[column], numers[:, column * DH : (column + 1) * DH], numer)
        attended = (numer / total).reshape(count, 8, DH)
        out_ref[start : start + count] = block_of(attended, lse.reshape(count, 8, 1))


def fold_kernel(first_ref, second_ref, *out_refs):
    parts = [first_ref[...].astype(F32), second_ref[...].astype(F32)]
    lses = [jnp.sum(part[:, 8:, :], -1, keepdims=True) for part in parts]
    peak = jnp.maximum(*lses)
    weights = [jnp.exp(lse - peak) for lse in lses]
    total = sum(weights)
    attended = sum(w * part[:, :8, :] for w, part in zip(weights, parts)) / total
    stats = spread(jnp.where(peak > LOW / 2, peak + jnp.log(total), LOW))
    result = jnp.concatenate([attended, stats], 1).astype(BF16)
    size = result.shape[0] // len(out_refs)
    for k, out_ref in enumerate(out_refs):
        out_ref[...] = result[k * size : (k + 1) * size]


def merge_kernel(spans_ref, here_ref, there_ref, out_ref):
    spans = spans_ref[...].astype(F32)
    attended = spans[:, :4].reshape(-1, 8, DH)
    row = jnp.broadcast_to(spans[:, 4, :1, :], attended.shape)
    kept = functools.reduce(jnp.logical_or, diagonals(attended.shape))
    lse = jnp.sum(jnp.where(kept, row, 0.0), -1, keepdims=True)
    tiles = [here_ref[0].astype(F32), there_ref[0].astype(F32)]
    lses = [jnp.sum(tile[8:], -1, keepdims=True) for tile in tiles]
    peak = functools.reduce(jnp.maximum, lses, jnp.max(lse, 0))
    weight = jnp.exp(lse - peak[None])
    weights = [jnp.exp(other - peak) for other in lses]
    total = sum(weights, jnp.sum(weight, 0))
    numer = sum(
        (w * tile[:8] for w, tile in zip(weights, tiles)), jnp.sum(weight * attended, 0)
    )
    result = numer / total
    out_ref[...] = jnp.concatenate([result[h : h + 1] for h in range(8)], 1).astype(BF16)


def vmem(count):
    return [pl.BlockSpec(memory_space=pltpu.VMEM)] * count


def hbm(count):
    return [pl.BlockSpec(memory_space=pltpu.HBM)] * count


def shards(
    queries,
    ctx_keys,
    ctx_values,
    lengths,
    new_key,
    new_value,
    span_keys,
    span_values,
    span_lists,
    span_slots,
):
    requests = lax.axis_size("span")
    chips = lax.axis_size("ctx") // CORES
    ch_dev = span_keys.shape[0]
    params = pltpu.CompilerParams(vmem_limit_bytes=16 * 1024 * 1024)
    alone = pltpu.CompilerParams(vmem_limit_bytes=56 * 1024 * 1024)
    blocks = jax.ShapeDtypeStruct((requests, 5, 2, DH), BF16)

    def tiles(count):
        return jax.ShapeDtypeStruct((count, 16, DH), BF16)

    def fold(here, there):
        return pl.pallas_call(
            fold_kernel,
            out_shape=[tiles(here.shape[0] // 2)] * 2,
            in_specs=vmem(2),
            out_specs=vmem(2),
            compiler_params=params,
            name="fold",
        )(here, there)

    packed = pl.pallas_call(
        pack_kernel,
        out_shape=blocks,
        in_specs=hbm(2),
        out_specs=hbm(1)[0],
        scratch_shapes=[
            pltpu.VMEM((requests // 4,) + blocks.shape[1:], BF16),
            pltpu.VMEM((1, KVH * DH), BF16),
            pltpu.VMEM(span_lists.shape, jnp.int32),
            pltpu.SemaphoreType.DMA((4,)),
        ],
        compiler_params=alone,
        name="pack",
    )(queries, span_lists)
    gathered = exchanged(packed)
    queries, span_keys, packed = lax.optimization_barrier((queries, span_keys, packed))
    table = span_slots.reshape(-1, min(DH, span_slots.shape[0]))
    fetched = (table, queries, new_key, new_value, ctx_keys, ctx_values)
    here, there, idents = pl.pallas_call(
        private_kernel,
        out_shape=[tiles(chips)] * CORES + [jax.ShapeDtypeStruct((ch_dev, DH), F32)],
        in_specs=hbm(1 + len(fetched)),
        out_specs=vmem(CORES + 1),
        scratch_shapes=[pltpu.SMEM(lengths.shape, jnp.int32)]
        + [pltpu.VMEM(array.shape, array.dtype) for array in fetched]
        + [pltpu.SemaphoreType.DMA((1 + len(fetched),))],
        compiler_params=alone,
        cost_estimate=pl.CostEstimate(
            flops=4 * HQ * ctx_keys.shape[1] * DH, bytes_accessed=1 << 20, transcendentals=1 << 14
        ),
        name="private",
    )(lengths, *fetched)
    there, gathered = lax.optimization_barrier((swapped(there, 1), gathered))
    turned = pl.pallas_call(
        turn_kernel,
        out_shape=jax.ShapeDtypeStruct((ch_dev * DH, span_keys.shape[1]), BF16),
        in_specs=vmem(1),
        out_specs=vmem(1)[0],
        compiler_params=params,
        name="turn",
    )(span_keys)
    partial = pl.pallas_call(
        span_kernel,
        out_shape=blocks,
        in_specs=vmem(4),
        out_specs=vmem(1)[0],
        compiler_params=params,
        cost_estimate=pl.CostEstimate(
            flops=4 * requests * 8 * DH * ch_dev * span_keys.shape[1],
            bytes_accessed=3 << 19,
            transcendentals=1 << 18,
        ),
        name="spans",
    )(gathered, idents, turned, span_values)
    partial = exchanged(partial)
    for mask in (1, 3):
        here, there = fold(here, there)
        there = swapped(there, mask * CORES)
    return pl.pallas_call(
        merge_kernel,
        out_shape=jax.ShapeDtypeStruct((1, KVH * DH), BF16),
        in_specs=vmem(3),
        out_specs=vmem(1)[0],
        compiler_params=params,
        name="merge",
    )(partial, here, there)


def solution(mesh):
    in_specs = (
        P("span", None),
        P("span", "ctx", None),
        P("span", "ctx", None),
        P("span"),
        P("span", "ctx"),
        P("span", "ctx"),
        P("span", None, "ctx"),
        P("span", None, "ctx"),
        P("span", None),
        P(),
    )
    out_specs = P("span", "ctx")
    return jax.shard_map(shards, mesh=mesh, in_specs=in_specs, out_specs=out_specs, check_vma=False)
```
